32 devices in a mesh: grp: 2 (over y), node: 4 (over z), feat: 2 (over x), sub: 2 (over core).
Axes of the slice: x: 2, y: 2, z: 4, core: 2. Of those that a mesh axis runs over, the one named last changes fastest.
Arguments:
- features: bfloat16 [16384, 128], P(('grp', 'node', 'sub'), 'feat'), parts along dimension 0, may hold values from -6 to 6
- adjacency: bfloat16 [128, 8, 128, 128], P(('grp', 'node', 'sub')), parts along dimension 0, may hold values from 0 to 0.099609375
- neighbors: int32 [128, 8], P(('grp', 'node', 'sub')), parts along dimension 0, may hold values from 0 to 63, as said below
- edge_mask: int32 [128, 8], P(('grp', 'node', 'sub')), parts along dimension 0, may hold values 0 or 1
- feature_mask: int32 [16384, 128], P(('grp', 'node', 'sub'), 'feat'), parts along dimension 0, may hold values 0 or 1
- weight: bfloat16 [128, 256], P(None, 'feat'), may hold values from -0.5 to 0.5
- cotangent: bfloat16 [16384, 256], P(('grp', 'node', 'sub'), 'feat'), parts along dimension 0, may hold values from -6 to 6
Outputs:
- hidden: bfloat16 [16384, 256], P(('grp', 'node', 'sub'), 'feat'), parts along dimension 0
- grad_weight: float32 [256, 256], P('grp', 'feat'), parts along dimension 0
- grad_features: bfloat16 [16384, 128], P(('grp', 'node', 'sub'), 'feat'), parts along dimension 0
The draws below stay inside these ranges and needn't reach their ends.
There are 2 independent parts, one for each index of `grp`. The reference program is written for one: setup_inputs(seed, part) draws one part's arguments, and reference() takes and returns one part's arrays. A program takes and returns all parts, laid end to end along the dimension named above; an argument that names none is the same for every part. Nothing has to cross between parts.
Inputs may be any that keep to these rules, and one draw needn't show every extreme that they name: `neighbors`: block c is held by owner device c // 8. Over the 64 entries of one device's row blocks, at most 9 entries name blocks of any one owner device.
All inputs are finite; a program needn't handle non-finite values. No bound on the sum of `edge_mask` or of `feature_mask` on one device may be relied on, other than what follows from the above.
Results may differ from the reference program's by a relative error of at most 0.017.
Values may be sent and summed in bfloat16 or wider, within the bound.
A program may use at most 64 MiB of HBM per device.

```python
import math
import jax
import jax.numpy as jnp

F = 128
HID = 256
BLK = 128
NB_DEV = 8
K = 8
OWNERS = 8
NBLK = 64
NODES = 8192
CAP = 9


def draw_neighbors(key, part):
    key = jax.random.fold_in(key, 7)
    hub_key, rest_key = jax.random.split(key)
    hub_owner = jax.random.randint(hub_key, (), 0, OWNERS).astype(jnp.int32)
    device_keys = jax.random.split(rest_key, OWNERS)
    entries = NB_DEV * K

    def one_device(dev_key, device):
        pool_key, mix_key, local_key = jax.random.split(dev_key, 3)
        second = jnp.where(hub_owner == device, (device + 1) % OWNERS, hub_owner).astype(jnp.int32)
        candidates = jnp.repeat(jnp.arange(OWNERS, dtype=jnp.int32), CAP)
        ranking = jax.random.permutation(pool_key, OWNERS * CAP).astype(jnp.int32)
        banned = ((candidates == device) | (candidates == second)).astype(jnp.int32)
        picked = candidates[jnp.argsort(banned * (OWNERS * CAP) + ranking)][:entries - 2 * CAP]
        owner_list = jnp.concatenate([jnp.full((CAP,), device, jnp.int32), jnp.full((CAP,), second, jnp.int32), picked])
        owner_list = jax.random.permutation(mix_key, owner_list)
        within = jax.random.randint(local_key, (entries,), 0, NB_DEV).astype(jnp.int32)
        return (owner_list * NB_DEV + within).reshape(NB_DEV, K)
    result = jax.vmap(one_device)(device_keys, jnp.arange(OWNERS, dtype=jnp.int32))
    return result.reshape(NBLK, K).astype(jnp.int32)


def place_ends(values, own_key, low, top_value):
    shape = values.shape
    spot = [jax.random.randint(jax.random.fold_in(own_key, axis), (), 0, shape[axis]) for axis in range(len(shape))]
    values = values.at[tuple(spot)].set(low)
    longest = shape.index(max(shape))
    spot[longest] = (spot[longest] + 1) % shape[longest]
    return values.at[tuple(spot)].set(top_value)


def level_of(stream_key, extent, cuts, low, top_value):
    def one(position, blocks):
        draws = jax.random.uniform(jax.random.fold_in(jax.random.fold_in(stream_key, 6), position), (blocks,), jnp.float32, low / len(cuts), top_value / len(cuts))
        return jnp.repeat(jnp.exp(draws), extent[position] // blocks).reshape((-1,) + (1,) * (len(extent) - position - 1))

    level = one(*cuts[0])
    for cut in cuts[1:]:
        level = level * one(*cut)
    return level


def scatter_about(own_key, extent, scale, most, pieces=(), kind=jnp.bfloat16):
    loudness = level_of(own_key, extent, pieces, -0.22, 0.18) if pieces else 1.0
    values = jax.random.normal(own_key, extent, jnp.float32) * scale * loudness
    return jnp.minimum(jnp.maximum(values, -most), most).astype(kind)


def setup_inputs(seed: int = 0, part: int = 0) -> dict:
    key_of = jax.random.split(jax.random.key(seed), 8)
    part_keys = jax.random.split(jax.random.fold_in(key_of[7], part), 8)
    return {
        "features": scatter_about(part_keys[0], (NODES, F), 1.0, 6.0, ((0, 8), (1, 2))),
        "adjacency": jnp.clip(0.099609375 * jax.random.uniform(part_keys[1], (NBLK, K, BLK, BLK), jnp.float32) ** level_of(part_keys[1], (NBLK, K, BLK, BLK), ((0, 8),), -0.2, 0.2), 0.0, 0.099609375).astype(jnp.bfloat16),
        "neighbors": draw_neighbors(jax.random.fold_in(jax.random.fold_in(key_of[7], part), 71), part),
        "edge_mask": place_ends((jax.random.randint(part_keys[3], (NBLK, K), 0, 4) < 3).astype(jnp.int32), jax.random.fold_in(part_keys[3], 1), 0, 1),
        "feature_mask": place_ends((jax.random.randint(part_keys[4], (NODES, F), 0, 2) < 1).astype(jnp.int32), jax.random.fold_in(part_keys[4], 1), 0, 1),
        "weight": scatter_about(key_of[5], (F, HID), F ** -0.5, 0.5, ((1, 2),)),
        "cotangent": scatter_about(part_keys[6], (NODES, HID), 1.0, 6.0, ((0, 8), (1, 2))),
    }


def activation(values):
    return jax.nn.gelu(values, approximate=True)

def reference(features, adjacency, neighbors, edge_mask, feature_mask, weight, cotangent):
    dropped = (features.astype(jnp.float32) * feature_mask.astype(jnp.float32) * 2.0).astype(jnp.bfloat16)
    masked = adjacency * edge_mask.astype(jnp.bfloat16)[:, :, None, None]
    needed = dropped.reshape(NBLK, BLK, F)[neighbors]
    summed = jnp.einsum('bkij,bkjf->bif', masked.astype(jnp.float32), needed.astype(jnp.float32))
    propagated = summed.reshape(NODES, F).astype(jnp.bfloat16)
    preact = jnp.dot(propagated, weight, preferred_element_type=jnp.float32)
    hidden = activation(preact).astype(jnp.bfloat16)
    _, pullback = jax.vjp(activation, preact)
    grad_pre = pullback(cotangent.astype(jnp.float32))[0].astype(jnp.bfloat16)
    grad_weight = jnp.dot(propagated.T, grad_pre, preferred_element_type=jnp.float32) * (1.0 / math.sqrt(NODES))
    grad_prop = jnp.dot(grad_pre, weight.T, preferred_element_type=jnp.float32).astype(jnp.bfloat16)
    block_terms = jnp.einsum('bkij,bif->bkjf', masked.astype(jnp.float32), grad_prop.reshape(NBLK, BLK, F).astype(jnp.float32)).astype(jnp.bfloat16)
    grad_dropped = jnp.zeros((NBLK, BLK, F), jnp.float32).at[neighbors.reshape(-1)].add(block_terms.reshape(-1, BLK, F).astype(jnp.float32))
    grad_features = (grad_dropped.reshape(NODES, F) * feature_mask.astype(jnp.float32) * 2.0).astype(jnp.bfloat16)
    return (hidden, grad_weight, grad_features)
```

```python
import functools
import math

import jax
import jax.numpy as jnp
from jax import lax
from jax.experimental import pallas as pl
from jax.experimental.pallas import tpu as pltpu
from jax.sharding import PartitionSpec as P

MESH = pl.DeviceIdType.MESH
CUBIC = 0.044715
SLOPE = math.sqrt(2.0 / math.pi)


def dot(a, b, ca, cb):
    return lax.dot_general(a, b, (((ca,), (cb,)), ((), ())), preferred_element_type=jnp.float32)


def kernel(
    chips, feats, blocks, per, cap, scale,
    nbr, keep_edge, slot_entry, slot_weight, slot_keep, block_end,
    feat_hbm, mask_hbm, adj_hbm, weight_hbm, cot_hbm,
    hidden_hbm, gw_hbm, gf_hbm,
    feat, fmask, adj, weight, cot, hid, gfo,
    rows, prop, gown, gsend, grecv, terms, runs,
    sown, soth, score, sup, sdown,
    gw, gw_send, gw_recv, gw_chip, gw_out,
    in_sem, out_sem,
    gu_s, gu_r, gd_s, gd_r, gc_s, gc_r,
    p_s, p_r, q_s, q_r,
    c_s, c_r, u_s, u_r, d_s, d_r,
    w_s, w_r, wz_s, wz_r, wo_s, wo_r,
):
    z = lax.axis_index("node")
    f = lax.axis_index("feat")
    q = lax.axis_index("sub")
    half, size = rows.shape[1], rows.shape[2]
    pairs = blocks // 2
    mid = gw.shape[1]

    def remote(src, dst, ss, rs, **where):
        return pltpu.make_async_remote_copy(
            src_ref=src, dst_ref=dst, send_sem=ss, recv_sem=rs,
            device_id=where, device_id_type=MESH,
        )

    def owner_rows(zz, core):
        return rows.at[pl.ds((zz * 2 + core) * blocks, blocks)]

    loads = [
        pltpu.make_async_copy(feat_hbm, feat, in_sem.at[0]),
        pltpu.make_async_copy(mask_hbm, fmask, in_sem.at[1]),
        pltpu.make_async_copy(adj_hbm, adj, in_sem.at[2]),
        pltpu.make_async_copy(cot_hbm, cot, in_sem.at[3]),
    ] + [
        pltpu.make_async_copy(weight_hbm.at[pl.ds(i * half, half)], weight.at[i], in_sem.at[4 + i])
        for i in range(feats)
    ]
    for copy in loads:
        copy.start()

    barrier = pltpu.get_barrier_semaphore()
    for d in range(1, feats):
        pl.semaphore_signal(
            barrier, inc=1, device_id={"feat": lax.rem(f + d, feats)}, device_id_type=MESH
        )
    pl.semaphore_signal(barrier, inc=1, device_id={"sub": 1 - q}, device_id_type=MESH)
    for d in range(1, chips):
        pl.semaphore_signal(
            barrier, inc=1, device_id={"node": lax.rem(z + d, chips)}, device_id_type=MESH
        )

    loads[0].wait()
    loads[1].wait()
    eye_f = (
        lax.broadcasted_iota(jnp.int32, (half, half), 0)
        == lax.broadcasted_iota(jnp.int32, (half, half), 1)
    ).astype(jnp.float32).astype(jnp.bfloat16)
    eye_n = (
        lax.broadcasted_iota(jnp.int32, (size, size), 0)
        == lax.broadcasted_iota(jnp.int32, (size, size), 1)
    ).astype(jnp.float32).astype(jnp.bfloat16)
    base = (z * 2 + q) * blocks
    for b in range(blocks):
        here = pl.ds(b * size, size)
        x = feat[here, :].astype(jnp.float32) * fmask[here, :].astype(jnp.float32) * 2.0
        rows[base + b] = dot(eye_f, x.astype(jnp.bfloat16), 1, 1).astype(jnp.bfloat16)

    pl.semaphore_wait(barrier, chips + feats - 1)

    def gather_up(zz):
        part = owner_rows(zz, q)
        return remote(part, part, gu_s.at[zz], gu_r.at[zz], node=lax.rem(z + 1, chips))

    def gather_down(zz):
        part = owner_rows(zz, q)
        return remote(part, part, gd_s.at[zz], gd_r.at[zz], node=lax.rem(z + chips - 1, chips))

    def gather_core(zz, core):
        part = owner_rows(zz, core)
        return remote(part, part, gc_s.at[zz], gc_r.at[zz], sub=1 - q)

    pl.when(z < chips - 1)(lambda: gather_up(z).start())
    pl.when(z > 0)(lambda: gather_down(z).start())
    gather_core(z, q).start()
    for d in range(1, chips):

        @pl.when(z - d >= 0)
        def _():
            gather_up(z - d).wait_recv()
            pl.when(z < chips - 1)(lambda: gather_up(z - d).start())
            gather_core(z - d, q).start()

        @pl.when(z + d < chips)
        def _():
            gather_down(z + d).wait_recv()
            pl.when(z > 0)(lambda: gather_down(z + d).start())
            gather_core(z + d, q).start()

    loads[2].wait()
    for zz in range(chips):
        gather_core(zz, 1 - q).wait_recv()

    def blocks_of(b):
        return jnp.concatenate([adj[b, k] for k in range(per)], axis=1)

    def send_prop(c, d):
        part = prop.at[f, pl.ds(2 * c, 2)]
        return remote(part, part, p_s.at[d, c], p_r.at[d, c], feat=lax.rem(f + d, feats))

    def recv_prop(c, d):
        part = prop.at[lax.rem(f + feats - d, feats), pl.ds(2 * c, 2)]
        return remote(part, part, p_s.at[d, c], p_r.at[d, c], feat=lax.rem(f + d, feats))

    for c in range(pairs):
        for b in (2 * c, 2 * c + 1):
            parts = []
            for k in range(per):
                e = b * per + k
                live = keep_edge[e].astype(jnp.float32)
                parts.append((rows[nbr[e]].astype(jnp.float32) * live).astype(jnp.bfloat16))
            prop[f, b] = dot(jnp.concatenate(parts, axis=1), blocks_of(b), 1, 1).astype(
                jnp.bfloat16
            )
        for d in range(1, feats):
            send_prop(c, d).start()

    for copy in loads[3:]:
        copy.wait()
    whole_weight = jnp.concatenate([weight[i] for i in range(feats)], axis=0)

    def send_grad(c, d):
        part = pl.ds(2 * c, 2)
        return remote(
            gsend.at[d, part], grecv.at[d, part], q_s.at[d, c], q_r.at[d, c],
            feat=lax.rem(f + d, feats),
        )

    def store_hidden(c):
        part = pl.ds(2 * c * size, 2 * size)
        return pltpu.make_async_copy(hid.at[part], hidden_hbm.at[part], out_sem.at[c])

    total = jnp.zeros((feats * half, weight.shape[2]), jnp.float32)
    for c in range(pairs):
        for d in range(1, feats):
            recv_prop(c, d).wait_recv()
        for b in (2 * c, 2 * c + 1):
            here = pl.ds(b * size, size)
            full = jnp.concatenate([prop[i, b] for i in range(feats)], axis=0)
            v = dot(full, whole_weight, 0, 0)
            square = v * v
            t = jnp.tanh(SLOPE * v * (1.0 + CUBIC * square))
            hid[here, :] = (0.5 * v * (1.0 + t)).astype(jnp.bfloat16)
            slope = 0.5 * (1.0 + t) + 0.5 * v * (1.0 - t * t) * (
                SLOPE * (1.0 + 3.0 * CUBIC * square)
            )
            gp = (cot[here, :].astype(jnp.float32) * slope).astype(jnp.bfloat16)
            total = total + dot(full, gp, 1, 0)
            gown[b] = dot(weight[f], gp, 1, 1)
            for d in range(1, feats):
                gsend[d, b] = dot(weight[lax.rem(f + d, feats)], gp, 1, 1).astype(jnp.bfloat16)
        for d in range(1, feats):
            send_grad(c, d).start()
        store_hidden(c).start()

    gw[0] = total[:mid]
    gw[1] = total[mid:]
    gw_send[...] = gw[1 - q]
    gw_swap = remote(gw_send, gw_recv, w_s, w_r, sub=1 - q)
    gw_swap.start()

    for c in range(pairs):
        for d in range(1, feats):
            send_grad(c, d).wait_recv()
        for b in (2 * c, 2 * c + 1):
            gsum = gown[b]
            for d in range(1, feats):
                gsum = gsum + grecv[d, b].astype(jnp.float32)
            gprop = gsum.astype(jnp.bfloat16)
            out = dot(gprop, blocks_of(b), 1, 0)
            for k in range(per):
                terms[b * per + k] = out[:, k * size:(k + 1) * size]

    gw_swap.wait_recv()
    gw_chip[z] = (gw[q] + gw_recv[...]).astype(jnp.bfloat16)

    def gw_to(d):
        return remote(
            gw_chip.at[z], gw_chip.at[z], wz_s.at[d], wz_r.at[d], node=lax.rem(z + d, chips)
        )

    def gw_from(d):
        part = gw_chip.at[lax.rem(z + chips - d, chips)]
        return remote(part, part, wz_s.at[d], wz_r.at[d], node=lax.rem(z + d, chips))

    for d in range(1, chips):
        gw_to(d).start()

    runs[cap] = jnp.zeros((half, size), jnp.float32)

    def sum_terms(zz, core, dest):
        owner = zz * 2 + core
        total = None
        for s in range(cap):
            p = owner * cap + s
            term = terms[slot_entry[p]] * slot_weight[p].astype(jnp.float32)
            total = term if s == 0 else total * slot_keep[p].astype(jnp.float32) + term
            runs[s] = total
        for i in range(blocks):
            dest[zz, i] = runs[block_end[owner * blocks + i]].astype(jnp.bfloat16)

    def core_copy(zz):
        return remote(soth.at[zz], score.at[zz], c_s.at[zz], c_r.at[zz], sub=1 - q)

    def up_copy(zz):
        return remote(sown.at[zz], sup.at[zz], u_s.at[zz], u_r.at[zz], node=lax.rem(z + 1, chips))

    def down_copy(zz):
        return remote(
            sown.at[zz], sdown.at[zz], d_s.at[zz], d_r.at[zz], node=lax.rem(z + chips - 1, chips)
        )

    def collect(zz):
        sum_terms(zz, 1 - q, soth)
        core_copy(zz).start()
        sum_terms(zz, q, sown)

    def join(zz, other):
        for i in range(blocks):
            sown[zz, i] = (
                sown[zz, i].astype(jnp.float32) + other[zz, i].astype(jnp.float32)
            ).astype(jnp.bfloat16)

    def forward_up(zz):
        core_copy(zz).wait_recv()
        join(zz, score)

        @pl.when(z > 0)
        def _():
            up_copy(zz).wait_recv()
            join(zz, sup)

        up_copy(zz).start()

    def forward_down(zz):
        core_copy(zz).wait_recv()
        join(zz, score)

        @pl.when(z < chips - 1)
        def _():
            down_copy(zz).wait_recv()
            join(zz, sdown)

        down_copy(zz).start()

    for t in range(chips):
        if t < chips - 1:
            pl.when(chips - 1 - t > z)(lambda: collect(chips - 1 - t))
            pl.when(t < z)(lambda: collect(t))
        if t > 0:
            pl.when(chips - t > z)(lambda: forward_up(chips - t))
            pl.when(t - 1 < z)(lambda: forward_down(t - 1))
    collect(z)

    for d in range(1, chips):
        gw_from(d).wait_recv()
    gw_sum = gw_chip[0].astype(jnp.float32)
    for zz in range(1, chips):
        gw_sum = gw_sum + gw_chip[zz].astype(jnp.float32)
    gw_out[q] = gw_sum * scale
    gw_share = remote(gw_out.at[q], gw_out.at[q], wo_s, wo_r, sub=1 - q)
    gw_share_back = remote(gw_out.at[1 - q], gw_out.at[1 - q], wo_s, wo_r, sub=1 - q)
    gw_share.start()

    core_copy(z).wait_recv()

    @pl.when(z > 0)
    def _():
        up_copy(z).wait_recv()

    @pl.when(z < chips - 1)
    def _():
        down_copy(z).wait_recv()

    has_up = z > 0
    has_down = z < chips - 1

    pl.when(jnp.logical_not(has_up))(lambda: sup.__setitem__(z, jnp.zeros_like(sup[z])))
    pl.when(jnp.logical_not(has_down))(lambda: sdown.__setitem__(z, jnp.zeros_like(sdown[z])))
    for b in range(blocks):
        here = pl.ds(b * size, size)
        grad = (
            sown[z, b].astype(jnp.float32)
            + score[z, b].astype(jnp.float32)
            + sup[z, b].astype(jnp.float32)
            + sdown[z, b].astype(jnp.float32)
        ).astype(jnp.bfloat16)
        back = dot(eye_n, grad, 1, 1)
        gfo[here, :] = (back * fmask[here, :].astype(jnp.float32) * 2.0).astype(jnp.bfloat16)
    gf_store = pltpu.make_async_copy(gfo, gf_hbm, out_sem.at[pairs])
    gf_store.start()
    gw_share_back.wait_recv()
    gw_stores = [
        pltpu.make_async_copy(gw_out.at[i], gw_hbm.at[pl.ds(i * mid, mid)], out_sem.at[pairs + 1 + i])
        for i in range(2)
    ]
    for copy in gw_stores:
        copy.start()

    for zz in range(chips):
        gather_core(zz, q).wait_send()
        core_copy(zz).wait_send()

        @pl.when(jnp.logical_and(zz <= z, z < chips - 1))
        def _():
            gather_up(zz).wait_send()

        @pl.when(jnp.logical_and(zz >= z, z > 0))
        def _():
            gather_down(zz).wait_send()

        pl.when(zz > z)(lambda: up_copy(zz).wait_send())
        pl.when(zz < z)(lambda: down_copy(zz).wait_send())
    for c in range(pairs):
        for d in range(1, feats):
            send_prop(c, d).wait_send()
            send_grad(c, d).wait_send()
        store_hidden(c).wait()
    gw_swap.wait_send()
    for d in range(1, chips):
        gw_to(d).wait_send()
    gw_share.wait_send()
    gf_store.wait()
    for copy in gw_stores:
        copy.wait()


def plan(neighbors, edge_mask, owners, blocks, cap):
    n = neighbors.reshape(-1)
    edge = edge_mask.reshape(-1)
    entries = n.shape[0]
    index = jnp.arange(entries, dtype=jnp.int32)
    owner = n // blocks
    same = owner[:, None] == owner[None, :]
    before = (n[None, :] < n[:, None]) | (
        (n[None, :] == n[:, None]) & (index[None, :] < index[:, None])
    )
    rank = jnp.sum((same & before).astype(jnp.int32), axis=1)
    place = owner * cap + rank
    slots = jnp.arange(owners * cap, dtype=jnp.int32)
    hit = (place[:, None] == slots[None, :]).astype(jnp.int32)
    slot_entry = jnp.sum(hit * index[:, None], axis=0)
    slot_weight = jnp.sum(hit * edge[:, None], axis=0)
    first = jnp.sum((same & (n[None, :] == n[:, None]) & before).astype(jnp.int32), axis=1) == 0
    slot_keep = jnp.sum(hit * (1 - first.astype(jnp.int32))[:, None], axis=0)
    names = jnp.arange(owners * blocks, dtype=jnp.int32)
    equal = jnp.sum((n[:, None] == names[None, :]).astype(jnp.int32), axis=0)
    upto = jnp.sum(
        ((owner[:, None] == (names // blocks)[None, :]) & (n[:, None] <= names[None, :])).astype(
            jnp.int32
        ),
        axis=0,
    )
    block_end = jnp.where(equal > 0, upto - 1, cap)
    return n, edge, slot_entry, slot_weight, slot_keep, block_end


def local(chips, features, adjacency, neighbors, edge_mask, feature_mask, weight, cotangent):
    rows_dev, half = features.shape
    blocks, per, size, _ = adjacency.shape
    owners = 2 * chips
    entries = blocks * per
    cap = entries // owners + 1
    total, hid = weight.shape
    feats = total // half
    mid = total // 2
    pairs = blocks // 2
    tables = plan(neighbors, edge_mask, owners, blocks, cap)
    bf, f32 = jnp.bfloat16, jnp.float32
    smem = pl.BlockSpec(memory_space=pltpu.SMEM)
    any_ = pl.BlockSpec(memory_space=pl.ANY)
    dma = pltpu.SemaphoreType.DMA
    body = functools.partial(
        kernel, chips, feats, blocks, per, cap, 1.0 / math.sqrt(rows_dev * owners)
    )
    return pl.pallas_call(
        body,
        out_shape=(
            jax.ShapeDtypeStruct((rows_dev, hid), bf),
            jax.ShapeDtypeStruct((total, hid), f32),
            jax.ShapeDtypeStruct((rows_dev, half), bf),
        ),
        in_specs=[smem] * 6 + [any_] * 5,
        out_specs=(any_, any_, any_),
        scratch_shapes=[
            pltpu.VMEM((rows_dev, half), bf),
            pltpu.VMEM((rows_dev, half), jnp.int32),
            pltpu.VMEM(adjacency.shape, bf),
            pltpu.VMEM((feats, half, hid), bf),
            pltpu.VMEM((rows_dev, hid), bf),
            pltpu.VMEM((rows_dev, hid), bf),
            pltpu.VMEM((rows_dev, half), bf),
            pltpu.VMEM((owners * blocks, half, size), bf),
            pltpu.VMEM((feats, blocks, half, size), bf),
            pltpu.VMEM((blocks, half, size), f32),
            pltpu.VMEM((feats, blocks, half, size), bf),
            pltpu.VMEM((feats, blocks, half, size), bf),
            pltpu.VMEM((entries, half, size), f32),
            pltpu.VMEM((cap + 1, half, size), f32),
        ]
        + [pltpu.VMEM((chips, blocks, half, size), bf)] * 5
        + [
            pltpu.VMEM((2, mid, hid), f32),
            pltpu.VMEM((mid, hid), f32),
            pltpu.VMEM((mid, hid), f32),
            pltpu.VMEM((chips, mid, hid), bf),
            pltpu.VMEM((2, mid, hid), f32),
            dma((4 + feats,)),
            dma((pairs + 3,)),
        ]
        + [dma((chips,))] * 6
        + [dma((feats, pairs))] * 4
        + [dma((chips,))] * 6
        + [dma, dma, dma((chips,)), dma((chips,)), dma, dma],
        compiler_params=pltpu.CompilerParams(
            collective_id=0, has_side_effects=True, vmem_limit_bytes=48 * 1024 * 1024
        ),
    )(*tables, features, feature_mask, adjacency, weight, cotangent)


def solution(mesh):
    split = ("grp", "node", "sub")
    in_specs = (
        P(split, "feat"),
        P(split, None, None, None),
        P(split, None),
        P(split, None),
        P(split, "feat"),
        P(None, "feat"),
        P(split, "feat"),
    )
    out_specs = (P(split, "feat"), P("grp", "feat"), P(split, "feat"))
    return jax.shard_map(
        functools.partial(local, mesh.shape["node"]),
        mesh=mesh, in_specs=in_specs, out_specs=out_specs, check_vma=False,
    )
```

```python
import functools
import math

import jax
import jax.numpy as jnp
from jax import lax
from jax.experimental import pallas as pl
from jax.experimental.pallas import tpu as pltpu
from jax.sharding import PartitionSpec as P

MESH = pl.DeviceIdType.MESH
CUBIC = 0.044715
SLOPE = math.sqrt(2.0 / math.pi)


def dot(a, b, ca, cb):
    return lax.dot_general(a, b, (((ca,), (cb,)), ((), ())), preferred_element_type=jnp.float32)


def kernel(
    chips, feats, blocks, per, cap, scale,
    nbr, keep_edge,
    feat_hbm, mask_hbm, adj_hbm, weight_hbm, cot_hbm,
    hidden_hbm, gw_hbm, gf_hbm,
    feat, fmask, adj, weight, cot, hid, gfo,
    rows, prop, gown, gsend, grecv, terms, runs,
    sown, soth, score, sup, sdown,
    gw, gw_send, gw_recv, gw_chip, gw_out,
    column, flags, table, tab, tab_sem,
    in_sem, out_sem,
    gu_s, gu_r, gd_s, gd_r, gc_s, gc_r,
    p_s, p_r, q_s, q_r,
    c_s, c_r, u_s, u_r, d_s, d_r,
    w_s, w_r, wz_s, wz_r, wo_s, wo_r,
):
    z = lax.axis_index("node")
    f = lax.axis_index("feat")
    q = lax.axis_index("sub")
    half, size = rows.shape[1], rows.shape[2]
    pairs = blocks // 2
    mid = gw.shape[1]

    def remote(src, dst, ss, rs, **where):
        return pltpu.make_async_remote_copy(
            src_ref=src, dst_ref=dst, send_sem=ss, recv_sem=rs,
            device_id=where, device_id_type=MESH,
        )

    def owner_rows(zz, core):
        return rows.at[pl.ds((zz * 2 + core) * blocks, blocks)]

    loads = [
        pltpu.make_async_copy(feat_hbm, feat, in_sem.at[0]),
        pltpu.make_async_copy(mask_hbm, fmask, in_sem.at[1]),
        pltpu.make_async_copy(adj_hbm, adj, in_sem.at[2]),
        pltpu.make_async_copy(cot_hbm, cot, in_sem.at[3]),
    ] + [
        pltpu.make_async_copy(weight_hbm.at[pl.ds(i * half, half)], weight.at[i], in_sem.at[4 + i])
        for i in range(feats)
    ]
    for copy in loads:
        copy.start()

    barrier = pltpu.get_barrier_semaphore()
    for d in range(1, feats):
        pl.semaphore_signal(
            barrier, inc=1, device_id={"feat": lax.rem(f + d, feats)}, device_id_type=MESH
        )
    pl.semaphore_signal(barrier, inc=1, device_id={"sub": 1 - q}, device_id_type=MESH)
    for d in range(1, chips):
        pl.semaphore_signal(
            barrier, inc=1, device_id={"node": lax.rem(z + d, chips)}, device_id_type=MESH
        )

    loads[0].wait()
    loads[1].wait()
    base = (z * 2 + q) * blocks
    for b in range(blocks):
        here = pl.ds(b * size, size)
        x = feat[:, here].astype(jnp.float32) * fmask[:, here].astype(jnp.float32) * 2.0
        rows[base + b] = x.astype(jnp.bfloat16)

    pl.semaphore_wait(barrier, chips + feats - 1)

    def gather_up(zz):
        part = owner_rows(zz, q)
        return remote(part, part, gu_s.at[zz], gu_r.at[zz], node=lax.rem(z + 1, chips))

    def gather_down(zz):
        part = owner_rows(zz, q)
        return remote(part, part, gd_s.at[zz], gd_r.at[zz], node=lax.rem(z + chips - 1, chips))

    def gather_core(zz, core):
        part = owner_rows(zz, core)
        return remote(part, part, gc_s.at[zz], gc_r.at[zz], sub=1 - q)

    pl.when(z < chips - 1)(lambda: gather_up(z).start())
    pl.when(z > 0)(lambda: gather_down(z).start())
    gather_core(z, q).start()
    make_tables(blocks, per, cap, nbr, keep_edge, column, flags, table)
    tab_copy = pltpu.make_async_copy(table, tab, tab_sem)
    tab_copy.start()
    for d in range(1, chips):

        @pl.when(z - d >= 0)
        def _():
            gather_up(z - d).wait_recv()
            pl.when(z < chips - 1)(lambda: gather_up(z - d).start())
            gather_core(z - d, q).start()

        @pl.when(z + d < chips)
        def _():
            gather_down(z + d).wait_recv()
            pl.when(z > 0)(lambda: gather_down(z + d).start())
            gather_core(z + d, q).start()

    loads[2].wait()
    tab_copy.wait()
    for zz in range(chips):
        gather_core(zz, 1 - q).wait_recv()

    def blocks_of(b):
        return jnp.concatenate([adj[b, k] for k in range(per)], axis=1)

    def send_prop(c, d):
        part = prop.at[f, pl.ds(2 * c, 2)]
        return remote(part, part, p_s.at[d, c], p_r.at[d, c], feat=lax.rem(f + d, feats))

    def recv_prop(c, d):
        part = prop.at[lax.rem(f + feats - d, feats), pl.ds(2 * c, 2)]
        return remote(part, part, p_s.at[d, c], p_r.at[d, c], feat=lax.rem(f + d, feats))

    for c in range(pairs):
        for b in (2 * c, 2 * c + 1):
            parts = []
            for k in range(per):
                live = keep_edge[b, k].astype(jnp.float32)
                parts.append((rows[nbr[b, k]].astype(jnp.float32) * live).astype(jnp.bfloat16))
            prop[f, b] = dot(jnp.concatenate(parts, axis=1), blocks_of(b), 1, 1).astype(
                jnp.bfloat16
            )
        for d in range(1, feats):
            send_prop(c, d).start()

    for copy in loads[3:]:
        copy.wait()
    whole_weight = jnp.concatenate([weight[i] for i in range(feats)], axis=0)

    def send_grad(c, d):
        part = pl.ds(2 * c, 2)
        return remote(
            gsend.at[d, part], grecv.at[d, part], q_s.at[d, c], q_r.at[d, c],
            feat=lax.rem(f + d, feats),
        )

    def store_hidden(c):
        part = pl.ds(2 * c * size, 2 * size)
        return pltpu.make_async_copy(hid.at[part], hidden_hbm.at[part], out_sem.at[c])

    total = jnp.zeros((feats * half, weight.shape[2]), jnp.float32)
    for c in range(pairs):
        for d in range(1, feats):
            recv_prop(c, d).wait_recv()
        for b in (2 * c, 2 * c + 1):
            here = pl.ds(b * size, size)
            full = jnp.concatenate([prop[i, b] for i in range(feats)], axis=0)
            v = dot(full, whole_weight, 0, 0)
            square = v * v
            t = jnp.tanh(SLOPE * v * (1.0 + CUBIC * square))
            hid[here, :] = (0.5 * v * (1.0 + t)).astype(jnp.bfloat16)
            slope = 0.5 * (1.0 + t) + 0.5 * v * (1.0 - t * t) * (
                SLOPE * (1.0 + 3.0 * CUBIC * square)
            )
            gp = (cot[here, :].astype(jnp.float32) * slope).astype(jnp.bfloat16)
            total = total + dot(full, gp, 1, 0)
            gown[b] = dot(weight[f], gp, 1, 1)
            for d in range(1, feats):
                gsend[d, b] = dot(weight[lax.rem(f + d, feats)], gp, 1, 1).astype(jnp.bfloat16)
        for d in range(1, feats):
            send_grad(c, d).start()
        store_hidden(c).start()

    gw[0] = total[:mid]
    gw[1] = total[mid:]
    gw_send[...] = gw[1 - q]
    gw_swap = remote(gw_send, gw_recv, w_s, w_r, sub=1 - q)
    gw_swap.start()

    for c in range(pairs):
        for d in range(1, feats):
            send_grad(c, d).wait_recv()
        for b in (2 * c, 2 * c + 1):
            gsum = gown[b]
            for d in range(1, feats):
                gsum = gsum + grecv[d, b].astype(jnp.float32)
            gprop = gsum.astype(jnp.bfloat16)
            out = dot(gprop, blocks_of(b), 1, 0)
            for k in range(per):
                terms[b * per + k] = out[:, k * size:(k + 1) * size]

    gw_swap.wait_recv()
    gw_chip[z] = (gw[q] + gw_recv[...]).astype(jnp.bfloat16)

    def gw_to(d):
        return remote(
            gw_chip.at[z], gw_chip.at[z], wz_s.at[d], wz_r.at[d], node=lax.rem(z + d, chips)
        )

    def gw_from(d):
        part = gw_chip.at[lax.rem(z + chips - d, chips)]
        return remote(part, part, wz_s.at[d], wz_r.at[d], node=lax.rem(z + d, chips))

    for d in range(1, chips):
        gw_to(d).start()

    runs[cap] = jnp.zeros((half, size), jnp.float32)

    def sum_terms(zz, core, dest):
        owner = zz * 2 + core
        total = None
        for s in range(cap):
            p = owner * cap + s
            term = terms[tab[0, p]] * tab[1, p].astype(jnp.float32)
            total = term if s == 0 else total * tab[2, p].astype(jnp.float32) + term
            runs[s] = total
        for i in range(blocks):
            dest[zz, i] = runs[tab[3, owner * blocks + i]].astype(jnp.bfloat16)

    def core_copy(zz):
        return remote(soth.at[zz], score.at[zz], c_s.at[zz], c_r.at[zz], sub=1 - q)

    def up_copy(zz):
        return remote(sown.at[zz], sup.at[zz], u_s.at[zz], u_r.at[zz], node=lax.rem(z + 1, chips))

    def down_copy(zz):
        return remote(
            sown.at[zz], sdown.at[zz], d_s.at[zz], d_r.at[zz], node=lax.rem(z + chips - 1, chips)
        )

    def collect(zz):
        sum_terms(zz, 1 - q, soth)
        core_copy(zz).start()
        sum_terms(zz, q, sown)

    def join(zz, other):
        for i in range(blocks):
            sown[zz, i] = (
                sown[zz, i].astype(jnp.float32) + other[zz, i].astype(jnp.float32)
            ).astype(jnp.bfloat16)

    def forward_up(zz):
        core_copy(zz).wait_recv()
        join(zz, score)

        @pl.when(z > 0)
        def _():
            up_copy(zz).wait_recv()
            join(zz, sup)

        up_copy(zz).start()

    def forward_down(zz):
        core_copy(zz).wait_recv()
        join(zz, score)

        @pl.when(z < chips - 1)
        def _():
            down_copy(zz).wait_recv()
            join(zz, sdown)

        down_copy(zz).start()

    for t in range(chips):
        if t < chips - 1:
            pl.when(chips - 1 - t > z)(lambda: collect(chips - 1 - t))
            pl.when(t < z)(lambda: collect(t))
        if t > 0:
            pl.when(chips - t > z)(lambda: forward_up(chips - t))
            pl.when(t - 1 < z)(lambda: forward_down(t - 1))
    collect(z)

    for d in range(1, chips):
        gw_from(d).wait_recv()
    gw_sum = gw_chip[0].astype(jnp.float32)
    for zz in range(1, chips):
        gw_sum = gw_sum + gw_chip[zz].astype(jnp.float32)
    gw_out[q] = gw_sum * scale
    gw_share = remote(gw_out.at[q], gw_out.at[q], wo_s, wo_r, sub=1 - q)
    gw_share_back = remote(gw_out.at[1 - q], gw_out.at[1 - q], wo_s, wo_r, sub=1 - q)
    gw_share.start()

    core_copy(z).wait_recv()

    @pl.when(z > 0)
    def _():
        up_copy(z).wait_recv()

    @pl.when(z < chips - 1)
    def _():
        down_copy(z).wait_recv()

    has_up = z > 0
    has_down = z < chips - 1

    pl.when(jnp.logical_not(has_up))(lambda: sup.__setitem__(z, jnp.zeros_like(sup[z])))
    pl.when(jnp.logical_not(has_down))(lambda: sdown.__setitem__(z, jnp.zeros_like(sdown[z])))
    for b in range(blocks):
        here = pl.ds(b * size, size)
        grad = (
            sown[z, b].astype(jnp.float32)
            + score[z, b].astype(jnp.float32)
            + sup[z, b].astype(jnp.float32)
            + sdown[z, b].astype(jnp.float32)
        )
        gfo[:, here] = (grad * fmask[:, here].astype(jnp.float32) * 2.0).astype(jnp.bfloat16)
    gf_store = pltpu.make_async_copy(gfo, gf_hbm, out_sem.at[pairs])
    gf_store.start()
    gw_share_back.wait_recv()
    gw_stores = [
        pltpu.make_async_copy(gw_out.at[i], gw_hbm.at[pl.ds(i * mid, mid)], out_sem.at[pairs + 1 + i])
        for i in range(2)
    ]
    for copy in gw_stores:
        copy.start()

    for zz in range(chips):
        gather_core(zz, q).wait_send()
        core_copy(zz).wait_send()

        @pl.when(jnp.logical_and(zz <= z, z < chips - 1))
        def _():
            gather_up(zz).wait_send()

        @pl.when(jnp.logical_and(zz >= z, z > 0))
        def _():
            gather_down(zz).wait_send()

        pl.when(zz > z)(lambda: up_copy(zz).wait_send())
        pl.when(zz < z)(lambda: down_copy(zz).wait_send())
    for c in range(pairs):
        for d in range(1, feats):
            send_prop(c, d).wait_send()
            send_grad(c, d).wait_send()
        store_hidden(c).wait()
    gw_swap.wait_send()
    for d in range(1, chips):
        gw_to(d).wait_send()
    gw_share.wait_send()
    gf_store.wait()
    for copy in gw_stores:
        copy.wait()


def make_tables(blocks, per, cap, nbr, keep_edge, column, flags, table):
    entries, lanes = column.shape
    width = table.shape[1]
    int_ = jnp.int32
    lane = lax.broadcasted_iota(int_, (1, lanes), 1)
    row = jnp.full((1, lanes), 1 << 20, int_)
    for e in range(entries):
        name = nbr[e // per, e % per]
        column[e:e + 1, :] = jnp.full((1, lanes), name, int_)
        flags[e:e + 1, :] = jnp.full((1, lanes), keep_edge[e // per, e % per], int_)
        row = jnp.where(lane == e, name, row)
    n = column[...]
    upper = lax.broadcasted_iota(int_, (entries, lanes), 1) < lax.broadcasted_iota(
        int_, (entries, lanes), 0
    )
    twin = (n == row) & upper
    below = (lax.div(n, blocks) == lax.div(row, blocks)) & (row < n)
    rank = jnp.sum(jnp.where(below | twin, 1, 0), axis=1, keepdims=True)
    twins = jnp.sum(jnp.where(twin, 1, 0), axis=1, keepdims=True)
    n = n[:, :1]
    owner = lax.div(n, blocks)
    place = owner * cap + rank
    slot = lax.broadcasted_iota(int_, (entries, width), 1)
    index = lax.broadcasted_iota(int_, (entries, width), 0)
    hit = place == slot
    entry = jnp.sum(jnp.where(hit, index, 0), axis=0, keepdims=True)
    table[0:1, :] = jnp.clip(entry, 0, entries - 1)
    table[1:2, :] = jnp.sum(jnp.where(hit, flags[:, :1], 0), axis=0, keepdims=True)
    table[2:3, :] = jnp.sum(jnp.where(hit & (twins > 0), 1, 0), axis=0, keepdims=True)
    equal = jnp.sum(jnp.where(n == slot, 1, 0), axis=0, keepdims=True)
    upto = jnp.sum(
        jnp.where((owner == lax.div(slot, blocks)) & (n <= slot), 1, 0), axis=0, keepdims=True
    )
    table[3:4, :] = jnp.where(equal > 0, jnp.clip(upto - 1, 0, cap), cap)
    table[4:8, :] = jnp.zeros((4, width), int_)


def local(chips, features, adjacency, neighbors, edge_mask, feature_mask, weight, cotangent):
    rows_dev, half = features.shape
    blocks, per, size, _ = adjacency.shape
    owners = 2 * chips
    entries = blocks * per
    cap = entries // owners + 1
    total, hid = weight.shape
    feats = total // half
    mid = total // 2
    pairs = blocks // 2
    lanes = -(-entries // 128) * 128
    width = -(-owners * max(blocks, cap) // 128) * 128
    bf, f32 = jnp.bfloat16, jnp.float32
    smem = pl.BlockSpec(memory_space=pltpu.SMEM)
    any_ = pl.BlockSpec(memory_space=pltpu.HBM)
    dma = pltpu.SemaphoreType.DMA
    body = functools.partial(
        kernel, chips, feats, blocks, per, cap, 1.0 / math.sqrt(rows_dev * owners)
    )
    hidden, grad_weight, grad_features = pl.pallas_call(
        body,
        out_shape=(
            jax.ShapeDtypeStruct((rows_dev, hid), bf),
            jax.ShapeDtypeStruct((total, hid), f32),
            jax.ShapeDtypeStruct((half, rows_dev), bf),
        ),
        in_specs=[smem] * 2 + [any_] * 5,
        out_specs=(any_, any_, any_),
        scratch_shapes=[
            pltpu.VMEM((half, rows_dev), bf),
            pltpu.VMEM((half, rows_dev), jnp.int32),
            pltpu.VMEM(adjacency.shape, bf),
            pltpu.VMEM((feats, half, hid), bf),
            pltpu.VMEM((rows_dev, hid), bf),
            pltpu.VMEM((rows_dev, hid), bf),
            pltpu.VMEM((half, rows_dev), bf),
            pltpu.VMEM((owners * blocks, half, size), bf),
            pltpu.VMEM((feats, blocks, half, size), bf),
            pltpu.VMEM((blocks, half, size), f32),
            pltpu.VMEM((feats, blocks, half, size), bf),
            pltpu.VMEM((feats, blocks, half, size), bf),
            pltpu.VMEM((entries, half, size), f32),
            pltpu.VMEM((cap + 1, half, size), f32),
        ]
        + [pltpu.VMEM((chips, blocks, half, size), bf)] * 5
        + [
            pltpu.VMEM((2, mid, hid), f32),
            pltpu.VMEM((mid, hid), f32),
            pltpu.VMEM((mid, hid), f32),
            pltpu.VMEM((chips, mid, hid), bf),
            pltpu.VMEM((2, mid, hid), f32),
            pltpu.VMEM((entries, lanes), jnp.int32),
            pltpu.VMEM((entries, lanes), jnp.int32),
            pltpu.VMEM((8, width), jnp.int32),
            pltpu.SMEM((8, width), jnp.int32),
            dma,
            dma((4 + feats,)),
            dma((pairs + 3,)),
        ]
        + [dma((chips,))] * 6
        + [dma((feats, pairs))] * 4
        + [dma((chips,))] * 6
        + [dma, dma, dma((chips,)), dma((chips,)), dma, dma],
        compiler_params=pltpu.CompilerParams(
            collective_id=0, has_side_effects=True, vmem_limit_bytes=62 * 1024 * 1024
        ),
    )(neighbors, edge_mask, features.T, feature_mask.T, adjacency, weight, cotangent)
    return hidden, grad_weight, grad_features.T


def solution(mesh):
    split = ("grp", "node", "sub")
    in_specs = (
        P(split, "feat"),
        P(split, None, None, None),
        P(split, None),
        P(split, None),
        P(split, "feat"),
        P(None, "feat"),
        P(split, "feat"),
    )
    out_specs = (P(split, "feat"), P("grp", "feat"), P(split, "feat"))
    return jax.shard_map(
        functools.partial(local, mesh.shape["node"]),
        mesh=mesh, in_specs=in_specs, out_specs=out_specs, check_vma=False,
    )
```

```python
import functools
import math

import jax
import jax.numpy as jnp
from jax import lax
from jax.experimental import pallas as pl
from jax.experimental.pallas import tpu as pltpu
from jax.sharding import PartitionSpec as P

MESH = pl.DeviceIdType.MESH
CUBIC = 0.044715
SLOPE = math.sqrt(2.0 / math.pi)


def dot(a, b, ca, cb):
    return lax.dot_general(a, b, (((ca,), (cb,)), ((), ())), preferred_element_type=jnp.float32)


def kernel(
    chips, feats, blocks, per, cap, scale,
    nbr, keep_edge,
    feat_hbm, mask_hbm, adj_hbm, weight_hbm, cot_hbm,
    hidden_hbm, gw_hbm, gf_hbm,
    feat, fmask, adj, weight, cot, hid, gfo,
    rows, prop, gown, gsend, grecv, terms, runs,
    sown, soth, score, landed,
    gw, gw_send, gw_recv, gw_chip, gw_out,
    column, flags, table, tab, tab_sem,
    in_sem, out_sem,
    g_s, g_r, gc_s, gc_r,
    p_s, p_r, q_s, q_r,
    c_s, c_r, r_s, r_r,
    w_s, w_r, wz_s, wz_r, wo_s, wo_r,
):
    z = lax.axis_index("node")
    f = lax.axis_index("feat")
    q = lax.axis_index("sub")
    half, size = rows.shape[1], rows.shape[2]
    pairs = blocks // 2
    mid = gw.shape[1]
    near = sorted(range(1, chips), key=lambda d: min(d, chips - d))
    far = near[::-1]

    def remote(src, dst, ss, rs, **where):
        return pltpu.make_async_remote_copy(
            src_ref=src, dst_ref=dst, send_sem=ss, recv_sem=rs,
            device_id=where, device_id_type=MESH,
        )

    def owner_rows(zz, core):
        return rows.at[pl.ds((zz * 2 + core) * blocks, blocks)]

    loads = [
        pltpu.make_async_copy(feat_hbm, feat, in_sem.at[0]),
        pltpu.make_async_copy(mask_hbm, fmask, in_sem.at[1]),
        pltpu.make_async_copy(adj_hbm, adj, in_sem.at[2]),
        pltpu.make_async_copy(cot_hbm, cot, in_sem.at[3]),
    ] + [
        pltpu.make_async_copy(weight_hbm.at[pl.ds(i * half, half)], weight.at[i], in_sem.at[4 + i])
        for i in range(feats)
    ]
    for copy in loads:
        copy.start()

    barrier = pltpu.get_barrier_semaphore()
    for d in range(1, feats):
        pl.semaphore_signal(
            barrier, inc=1, device_id={"feat": lax.rem(f + d, feats)}, device_id_type=MESH
        )
    pl.semaphore_signal(barrier, inc=1, device_id={"sub": 1 - q}, device_id_type=MESH)
    for d in range(1, chips):
        pl.semaphore_signal(
            barrier, inc=1, device_id={"node": lax.rem(z + d, chips)}, device_id_type=MESH
        )

    loads[0].wait()
    loads[1].wait()
    base = (z * 2 + q) * blocks
    for b in range(blocks):
        here = pl.ds(b * size, size)
        x = feat[:, here].astype(jnp.float32) * fmask[:, here].astype(jnp.float32) * 2.0
        rows[base + b] = x.astype(jnp.bfloat16)

    pl.semaphore_wait(barrier, chips + feats - 1)

    def gather_to(d):
        part = owner_rows(z, q)
        return remote(part, part, g_s.at[d], g_r.at[d], node=lax.rem(z + d, chips))

    def gather_from(d):
        part = owner_rows(lax.rem(z + chips - d, chips), q)
        return remote(part, part, g_s.at[d], g_r.at[d], node=lax.rem(z + d, chips))

    def gather_core(zz, core):
        part = owner_rows(zz, core)
        return remote(part, part, gc_s.at[zz], gc_r.at[zz], sub=1 - q)

    for d in far:
        gather_to(d).start()
    gather_core(z, q).start()
    make_tables(blocks, per, cap, nbr, keep_edge, column, flags, table)
    tab_copy = pltpu.make_async_copy(table, tab, tab_sem)
    tab_copy.start()
    for d in near:
        gather_from(d).wait_recv()
        gather_core(lax.rem(z + chips - d, chips), q).start()

    loads[2].wait()
    tab_copy.wait()
    for zz in range(chips):
        gather_core(zz, 1 - q).wait_recv()

    def blocks_of(b):
        return jnp.concatenate([adj[b, k] for k in range(per)], axis=1)

    def send_prop(c, d):
        part = prop.at[f, pl.ds(2 * c, 2)]
        return remote(part, part, p_s.at[d, c], p_r.at[d, c], feat=lax.rem(f + d, feats))

    def recv_prop(c, d):
        part = prop.at[lax.rem(f + feats - d, feats), pl.ds(2 * c, 2)]
        return remote(part, part, p_s.at[d, c], p_r.at[d, c], feat=lax.rem(f + d, feats))

    for c in range(pairs):
        for b in (2 * c, 2 * c + 1):
            parts = []
            for k in range(per):
                live = keep_edge[b, k].astype(jnp.float32)
                parts.append((rows[nbr[b, k]].astype(jnp.float32) * live).astype(jnp.bfloat16))
            prop[f, b] = dot(jnp.concatenate(parts, axis=1), blocks_of(b), 1, 1).astype(
                jnp.bfloat16
            )
        for d in range(1, feats):
            send_prop(c, d).start()

    for copy in loads[3:]:
        copy.wait()
    whole_weight = jnp.concatenate([weight[i] for i in range(feats)], axis=0)

    def send_grad(c, d):
        part = pl.ds(2 * c, 2)
        return remote(
            gsend.at[d, part], grecv.at[d, part], q_s.at[d, c], q_r.at[d, c],
            feat=lax.rem(f + d, feats),
        )

    def store_hidden(c):
        part = pl.ds(2 * c * size, 2 * size)
        return pltpu.make_async_copy(hid.at[part], hidden_hbm.at[part], out_sem.at[c])

    total = jnp.zeros((feats * half, weight.shape[2]), jnp.float32)
    for c in range(pairs):
        for d in range(1, feats):
            recv_prop(c, d).wait_recv()
        for b in (2 * c, 2 * c + 1):
            here = pl.ds(b * size, size)
            full = jnp.concatenate([prop[i, b] for i in range(feats)], axis=0)
            v = dot(full, whole_weight, 0, 0)
            square = v * v
            t = jnp.tanh(SLOPE * v * (1.0 + CUBIC * square))
            hid[here, :] = (0.5 * v * (1.0 + t)).astype(jnp.bfloat16)
            slope = 0.5 * (1.0 + t) + 0.5 * v * (1.0 - t * t) * (
                SLOPE * (1.0 + 3.0 * CUBIC * square)
            )
            gp = (cot[here, :].astype(jnp.float32) * slope).astype(jnp.bfloat16)
            total = total + dot(full, gp, 1, 0)
            gown[b] = dot(weight[f], gp, 1, 1)
            for d in range(1, feats):
                gsend[d, b] = dot(weight[lax.rem(f + d, feats)], gp, 1, 1).astype(jnp.bfloat16)
        for d in range(1, feats):
            send_grad(c, d).start()
        store_hidden(c).start()

    gw[0] = total[:mid]
    gw[1] = total[mid:]
    gw_send[...] = gw[1 - q]
    gw_swap = remote(gw_send, gw_recv, w_s, w_r, sub=1 - q)
    gw_swap.start()

    for c in range(pairs):
        for d in range(1, feats):
            send_grad(c, d).wait_recv()
        for b in (2 * c, 2 * c + 1):
            gsum = gown[b]
            for d in range(1, feats):
                gsum = gsum + grecv[d, b].astype(jnp.float32)
            gprop = gsum.astype(jnp.bfloat16)
            out = dot(gprop, blocks_of(b), 1, 0)
            for k in range(per):
                terms[b * per + k] = out[:, k * size:(k + 1) * size]

    gw_swap.wait_recv()
    gw_chip[z] = (gw[q] + gw_recv[...]).astype(jnp.bfloat16)

    def gw_to(d):
        return remote(
            gw_chip.at[z], gw_chip.at[z], wz_s.at[d], wz_r.at[d], node=lax.rem(z + d, chips)
        )

    def gw_from(d):
        part = gw_chip.at[lax.rem(z + chips - d, chips)]
        return remote(part, part, wz_s.at[d], wz_r.at[d], node=lax.rem(z + d, chips))

    for d in range(1, chips):
        gw_to(d).start()

    runs[cap] = jnp.zeros((half, size), jnp.float32)

    def sum_terms(zz, core, dest):
        owner = zz * 2 + core
        total = None
        for s in range(cap):
            p = owner * cap + s
            term = terms[tab[0, p]] * tab[1, p].astype(jnp.float32)
            total = term if s == 0 else total * tab[2, p].astype(jnp.float32) + term
            runs[s] = total
        for i in range(blocks):
            dest[zz, i] = runs[tab[3, owner * blocks + i]].astype(jnp.bfloat16)

    def core_copy(zz):
        return remote(soth.at[zz], score.at[zz], c_s.at[zz], c_r.at[zz], sub=1 - q)

    def part_to(d):
        return remote(
            sown.at[lax.rem(z + d, chips)], landed.at[d], r_s.at[d], r_r.at[d],
            node=lax.rem(z + d, chips),
        )

    def collect(zz):
        sum_terms(zz, 1 - q, soth)
        core_copy(zz).start()
        sum_terms(zz, q, sown)

    def pass_on(d):
        zz = lax.rem(z + d, chips)
        core_copy(zz).wait_recv()
        for i in range(blocks):
            sown[zz, i] = (
                sown[zz, i].astype(jnp.float32) + score[zz, i].astype(jnp.float32)
            ).astype(jnp.bfloat16)
        part_to(d).start()

    for t, d in enumerate(far):
        collect(lax.rem(z + d, chips))
        if t > 0:
            pass_on(far[t - 1])
    collect(z)
    pass_on(far[-1])

    for d in range(1, chips):
        gw_from(d).wait_recv()
    gw_sum = gw_chip[0].astype(jnp.float32)
    for zz in range(1, chips):
        gw_sum = gw_sum + gw_chip[zz].astype(jnp.float32)
    gw_out[q] = gw_sum * scale
    gw_share = remote(gw_out.at[q], gw_out.at[q], wo_s, wo_r, sub=1 - q)
    gw_share_back = remote(gw_out.at[1 - q], gw_out.at[1 - q], wo_s, wo_r, sub=1 - q)
    gw_share.start()

    core_copy(z).wait_recv()

    for d in near:
        part_to(d).wait_recv()
    for b in range(blocks):
        here = pl.ds(b * size, size)
        grad = sown[z, b].astype(jnp.float32) + score[z, b].astype(jnp.float32)
        for d in range(1, chips):
            grad = grad + landed[d, b].astype(jnp.float32)
        gfo[:, here] = (grad * fmask[:, here].astype(jnp.float32) * 2.0).astype(jnp.bfloat16)
    gf_store = pltpu.make_async_copy(gfo, gf_hbm, out_sem.at[pairs])
    gf_store.start()
    gw_share_back.wait_recv()
    gw_stores = [
        pltpu.make_async_copy(gw_out.at[i], gw_hbm.at[pl.ds(i * mid, mid)], out_sem.at[pairs + 1 + i])
        for i in range(2)
    ]
    for copy in gw_stores:
        copy.start()

    for zz in range(chips):
        gather_core(zz, q).wait_send()
        core_copy(zz).wait_send()
    for d in range(1, chips):
        gather_to(d).wait_send()
        part_to(d).wait_send()
    for c in range(pairs):
        for d in range(1, feats):
            send_prop(c, d).wait_send()
            send_grad(c, d).wait_send()
        store_hidden(c).wait()
    gw_swap.wait_send()
    for d in range(1, chips):
        gw_to(d).wait_send()
    gw_share.wait_send()
    gf_store.wait()
    for copy in gw_stores:
        copy.wait()


def make_tables(blocks, per, cap, nbr, keep_edge, column, flags, table):
    entries, lanes = column.shape
    width = table.shape[1]
    int_ = jnp.int32
    lane = lax.broadcasted_iota(int_, (1, lanes), 1)
    row = jnp.full((1, lanes), 1 << 20, int_)
    for e in range(entries):
        name = nbr[e // per, e % per]
        column[e:e + 1, :] = jnp.full((1, lanes), name, int_)
        flags[e:e + 1, :] = jnp.full((1, lanes), keep_edge[e // per, e % per], int_)
        row = jnp.where(lane == e, name, row)
    n = column[...]
    upper = lax.broadcasted_iota(int_, (entries, lanes), 1) < lax.broadcasted_iota(
        int_, (entries, lanes), 0
    )
    twin = (n == row) & upper
    below = (lax.div(n, blocks) == lax.div(row, blocks)) & (row < n)
    rank = jnp.sum(jnp.where(below | twin, 1, 0), axis=1, keepdims=True)
    twins = jnp.sum(jnp.where(twin, 1, 0), axis=1, keepdims=True)
    n = n[:, :1]
    owner = lax.div(n, blocks)
    place = owner * cap + rank
    slot = lax.broadcasted_iota(int_, (entries, width), 1)
    index = lax.broadcasted_iota(int_, (entries, width), 0)
    hit = place == slot
    entry = jnp.sum(jnp.where(hit, index, 0), axis=0, keepdims=True)
    table[0:1, :] = jnp.clip(entry, 0, entries - 1)
    table[1:2, :] = jnp.sum(jnp.where(hit, flags[:, :1], 0), axis=0, keepdims=True)
    table[2:3, :] = jnp.sum(jnp.where(hit & (twins > 0), 1, 0), axis=0, keepdims=True)
    equal = jnp.sum(jnp.where(n == slot, 1, 0), axis=0, keepdims=True)
    upto = jnp.sum(
        jnp.where((owner == lax.div(slot, blocks)) & (n <= slot), 1, 0), axis=0, keepdims=True
    )
    table[3:4, :] = jnp.where(equal > 0, jnp.clip(upto - 1, 0, cap), cap)
    table[4:8, :] = jnp.zeros((4, width), int_)


def store_results(a, b, c, a_out, b_out, c_out, sem):
    copies = [
        pltpu.make_async_copy(src, dst, sem.at[i])
        for i, (src, dst) in enumerate(((a, a_out), (b, b_out), (c, c_out)))
    ]
    for copy in copies:
        copy.start()
    for copy in copies:
        copy.wait()


def local(chips, features, adjacency, neighbors, edge_mask, feature_mask, weight, cotangent):
    rows_dev, half = features.shape
    blocks, per, size, _ = adjacency.shape
    owners = 2 * chips
    entries = blocks * per
    cap = entries // owners + 1
    total, hid = weight.shape
    feats = total // half
    mid = total // 2
    pairs = blocks // 2
    lanes = -(-entries // 128) * 128
    width = -(-owners * max(blocks, cap) // 128) * 128
    bf, f32 = jnp.bfloat16, jnp.float32
    smem = pl.BlockSpec(memory_space=pltpu.SMEM)
    any_ = pl.BlockSpec(memory_space=pltpu.HBM)
    dma = pltpu.SemaphoreType.DMA
    body = functools.partial(
        kernel, chips, feats, blocks, per, cap, 1.0 / math.sqrt(rows_dev * owners)
    )
    hidden, grad_weight, grad_features = pl.pallas_call(
        body,
        out_shape=(
            jax.ShapeDtypeStruct((rows_dev, hid), bf),
            jax.ShapeDtypeStruct((total, hid), f32),
            jax.ShapeDtypeStruct((half, rows_dev), bf),
        ),
        in_specs=[smem] * 2 + [any_] * 5,
        out_specs=(any_, any_, any_),
        scratch_shapes=[
            pltpu.VMEM((half, rows_dev), bf),
            pltpu.VMEM((half, rows_dev), jnp.int32),
            pltpu.VMEM(adjacency.shape, bf),
            pltpu.VMEM((feats, half, hid), bf),
            pltpu.VMEM((rows_dev, hid), bf),
            pltpu.VMEM((rows_dev, hid), bf),
            pltpu.VMEM((half, rows_dev), bf),
            pltpu.VMEM((owners * blocks, half, size), bf),
            pltpu.VMEM((feats, blocks, half, size), bf),
            pltpu.VMEM((blocks, half, size), f32),
            pltpu.VMEM((feats, blocks, half, size), bf),
            pltpu.VMEM((feats, blocks, half, size), bf),
            pltpu.VMEM((entries, half, size), f32),
            pltpu.VMEM((cap + 1, half, size), f32),
        ]
        + [pltpu.VMEM((chips, blocks, half, size), bf)] * 4
        + [
            pltpu.VMEM((2, mid, hid), f32),
            pltpu.VMEM((mid, hid), f32),
            pltpu.VMEM((mid, hid), f32),
            pltpu.VMEM((chips, mid, hid), bf),
            pltpu.VMEM((2, mid, hid), f32),
            pltpu.VMEM((entries, lanes), jnp.int32),
            pltpu.VMEM((entries, lanes), jnp.int32),
            pltpu.VMEM((8, width), jnp.int32),
            pltpu.SMEM((8, width), jnp.int32),
            dma,
            dma((4 + feats,)),
            dma((pairs + 3,)),
        ]
        + [dma((chips,))] * 4
        + [dma((feats, pairs))] * 4
        + [dma((chips,))] * 4
        + [dma, dma, dma((chips,)), dma((chips,)), dma, dma],
        compiler_params=pltpu.CompilerParams(
            collective_id=0, has_side_effects=True, vmem_limit_bytes=62 * 1024 * 1024
        ),
    )(neighbors, edge_mask, features.T, feature_mask.T, adjacency, weight, cotangent)
    results = (hidden, grad_weight, grad_features)
    hidden, grad_weight, grad_features = pl.pallas_call(
        store_results,
        out_shape=[jax.ShapeDtypeStruct(r.shape, r.dtype) for r in results],
        in_specs=[any_] * 3,
        out_specs=[any_] * 3,
        scratch_shapes=[dma((3,))],
        compiler_params=pltpu.CompilerParams(vmem_limit_bytes=62 * 1024 * 1024),
    )(*results)
    return hidden, grad_weight, grad_features.T


def solution(mesh):
    split = ("grp", "node", "sub")
    in_specs = (
        P(split, "feat"),
        P(split, None, None, None),
        P(split, None),
        P(split, None),
        P(split, "feat"),
        P(None, "feat"),
        P(split, "feat"),
    )
    out_specs = (P(split, "feat"), P("grp", "feat"), P(split, "feat"))
    return jax.shard_map(
        functools.partial(local, mesh.shape["node"]),
        mesh=mesh, in_specs=in_specs, out_specs=out_specs, check_vma=False,
    )
```

```python
import functools
import math

import jax
import jax.numpy as jnp
from jax import lax
from jax.experimental import pallas as pl
from jax.experimental.pallas import tpu as pltpu
from jax.sharding import PartitionSpec as P

MESH = pl.DeviceIdType.MESH
CUBIC = 0.044715
SLOPE = math.sqrt(2.0 / math.pi)


def dot(a, b, ca, cb):
    return lax.dot_general(a, b, (((ca,), (cb,)), ((), ())), preferred_element_type=jnp.float32)


def kernel(
    chips, feats, blocks, per, cap, scale,
    nbr, keep_edge,
    feat_hbm, mask_hbm, adj_hbm, weight_hbm, cot_hbm,
    hidden_hbm, gw_hbm, gf_hbm,
    feat, fmask, adj, weight, cot, hid, gfo,
    rows, prop, gown, gsend, grecv, terms, runs,
    sown, soth, score, landed,
    gw, gw_send, gw_recv, gw_chip, gw_out,
    column, flags, table, tab, tab_sem,
    in_sem, out_sem,
    g_s, g_r, gc_s, gc_r,
    p_s, p_r, q_s, q_r,
    c_s, c_r, r_s, r_r,
    w_s, w_r, wz_s, wz_r, wo_s, wo_r,
):
    z = lax.axis_index("node")
    f = lax.axis_index("feat")
    q = lax.axis_index("sub")
    half, size = rows.shape[1], rows.shape[2]
    pairs = blocks // 2
    mid = gw.shape[1]
    near = sorted(range(1, chips), key=lambda d: min(d, chips - d))
    far = near[::-1]

    def remote(src, dst, ss, rs, **where):
        return pltpu.make_async_remote_copy(
            src_ref=src, dst_ref=dst, send_sem=ss, recv_sem=rs,
            device_id=where, device_id_type=MESH,
        )

    def owner_rows(zz, core):
        return rows.at[pl.ds((zz * 2 + core) * blocks, blocks)]

    loads = [
        pltpu.make_async_copy(feat_hbm, feat, in_sem.at[0]),
        pltpu.make_async_copy(mask_hbm, fmask, in_sem.at[1]),
        pltpu.make_async_copy(adj_hbm, adj, in_sem.at[2]),
        pltpu.make_async_copy(cot_hbm, cot, in_sem.at[3]),
    ] + [
        pltpu.make_async_copy(weight_hbm.at[pl.ds(i * half, half)], weight.at[i], in_sem.at[4 + i])
        for i in range(feats)
    ]
    for copy in loads:
        copy.start()

    barrier = pltpu.get_barrier_semaphore()
    for d in range(1, feats):
        pl.semaphore_signal(
            barrier, inc=1, device_id={"feat": lax.rem(f + d, feats)}, device_id_type=MESH
        )
    pl.semaphore_signal(barrier, inc=1, device_id={"sub": 1 - q}, device_id_type=MESH)
    for d in range(1, chips):
        pl.semaphore_signal(
            barrier, inc=1, device_id={"node": lax.rem(z + d, chips)}, device_id_type=MESH
        )

    loads[0].wait()
    loads[1].wait()
    base = (z * 2 + q) * blocks
    for b in range(blocks):
        here = pl.ds(b * size, size)
        x = feat[:, here].astype(jnp.float32) * fmask[:, here].astype(jnp.float32) * 2.0
        rows[base + b] = x.astype(jnp.bfloat16)

    pl.semaphore_wait(barrier, chips + feats - 1)

    def gather_to(d):
        part = owner_rows(z, q)
        return remote(part, part, g_s.at[d], g_r.at[d], node=lax.rem(z + d, chips))

    def gather_from(d):
        part = owner_rows(lax.rem(z + chips - d, chips), q)
        return remote(part, part, g_s.at[d], g_r.at[d], node=lax.rem(z + d, chips))

    def gather_core(zz, core):
        part = owner_rows(zz, core)
        return remote(part, part, gc_s.at[zz], gc_r.at[zz], sub=1 - q)

    for d in far:
        gather_to(d).start()
    gather_core(z, q).start()
    make_tables(blocks, per, cap, nbr, keep_edge, column, flags, table)
    tab_copy = pltpu.make_async_copy(table, tab, tab_sem)
    tab_copy.start()
    for d in near:
        gather_from(d).wait_recv()
        gather_core(lax.rem(z + chips - d, chips), q).start()

    loads[2].wait()
    tab_copy.wait()
    for zz in range(chips):
        gather_core(zz, 1 - q).wait_recv()

    def blocks_of(b):
        return jnp.concatenate([adj[b, k] for k in range(per)], axis=1)

    def send_prop(c, d):
        part = prop.at[f, pl.ds(2 * c, 2)]
        return remote(part, part, p_s.at[d, c], p_r.at[d, c], feat=lax.rem(f + d, feats))

    def recv_prop(c, d):
        part = prop.at[lax.rem(f + feats - d, feats), pl.ds(2 * c, 2)]
        return remote(part, part, p_s.at[d, c], p_r.at[d, c], feat=lax.rem(f + d, feats))

    for c in range(pairs):
        for b in (2 * c, 2 * c + 1):
            parts = []
            for k in range(per):
                live = keep_edge[b, k].astype(jnp.float32)
                parts.append((rows[nbr[b, k]].astype(jnp.float32) * live).astype(jnp.bfloat16))
            prop[f, b] = dot(jnp.concatenate(parts, axis=1), blocks_of(b), 1, 1).astype(
                jnp.bfloat16
            )
        for d in range(1, feats):
            send_prop(c, d).start()

    for copy in loads[3:]:
        copy.wait()
    whole_weight = jnp.concatenate([weight[i] for i in range(feats)], axis=0)

    def send_grad(c, d):
        part = pl.ds(2 * c, 2)
        return remote(
            gsend.at[d, part], grecv.at[d, part], q_s.at[d, c], q_r.at[d, c],
            feat=lax.rem(f + d, feats),
        )

    def store_hidden(c):
        part = pl.ds(2 * c * size, 2 * size)
        return pltpu.make_async_copy(hid.at[part], hidden_hbm.at[part], out_sem.at[c])

    total = jnp.zeros((feats * half, weight.shape[2]), jnp.float32)
    for c in range(pairs):
        for d in range(1, feats):
            recv_prop(c, d).wait_recv()
        for b in (2 * c, 2 * c + 1):
            here = pl.ds(b * size, size)
            full = jnp.concatenate([prop[i, b] for i in range(feats)], axis=0)
            v = dot(full, whole_weight, 0, 0)
            square = v * v
            t = jnp.tanh(SLOPE * v * (1.0 + CUBIC * square))
            hid[here, :] = (0.5 * v * (1.0 + t)).astype(jnp.bfloat16)
            slope = 0.5 * (1.0 + t) + 0.5 * v * (1.0 - t * t) * (
                SLOPE * (1.0 + 3.0 * CUBIC * square)
            )
            gp = (cot[here, :].astype(jnp.float32) * slope).astype(jnp.bfloat16)
            total = total + dot(full, gp, 1, 0)
            gown[b] = dot(weight[f], gp, 1, 1)
            for d in range(1, feats):
                gsend[d, b] = dot(weight[lax.rem(f + d, feats)], gp, 1, 1).astype(jnp.bfloat16)
        for d in range(1, feats):
            send_grad(c, d).start()
        store_hidden(c).start()

    gw[0] = total[:mid]
    gw[1] = total[mid:]
    gw_send[...] = gw[1 - q]
    gw_swap = remote(gw_send, gw_recv, w_s, w_r, sub=1 - q)
    gw_swap.start()

    for c in range(pairs):
        for d in range(1, feats):
            send_grad(c, d).wait_recv()
        for b in (2 * c, 2 * c + 1):
            gsum = gown[b]
            for d in range(1, feats):
                gsum = gsum + grecv[d, b].astype(jnp.float32)
            gprop = gsum.astype(jnp.bfloat16)
            out = dot(gprop, blocks_of(b), 1, 0)
            for k in range(per):
                terms[b * per + k] = out[:, k * size:(k + 1) * size]

    gw_swap.wait_recv()
    gw_chip[z] = (gw[q] + gw_recv[...]).astype(jnp.bfloat16)

    def gw_to(d):
        return remote(
            gw_chip.at[z], gw_chip.at[z], wz_s.at[d], wz_r.at[d], node=lax.rem(z + d, chips)
        )

    def gw_from(d):
        part = gw_chip.at[lax.rem(z + chips - d, chips)]
        return remote(part, part, wz_s.at[d], wz_r.at[d], node=lax.rem(z + d, chips))

    for d in range(1, chips):
        gw_to(d).start()

    runs[cap] = jnp.zeros((half, size), jnp.float32)

    def sum_terms(zz, core, dest):
        owner = zz * 2 + core
        total = None
        for s in range(cap):
            p = owner * cap + s
            term = terms[tab[0, p]] * tab[1, p].astype(jnp.float32)
            total = term if s == 0 else total * tab[2, p].astype(jnp.float32) + term
            runs[s] = total
        for i in range(blocks):
            dest[zz, i] = runs[tab[3, owner * blocks + i]].astype(jnp.bfloat16)

    def core_copy(zz):
        return remote(soth.at[zz], score.at[zz], c_s.at[zz], c_r.at[zz], sub=1 - q)

    def part_to(d):
        return remote(
            sown.at[lax.rem(z + d, chips)], landed.at[d], r_s.at[d], r_r.at[d],
            node=lax.rem(z + d, chips),
        )

    def collect(zz):
        sum_terms(zz, 1 - q, soth)
        core_copy(zz).start()
        sum_terms(zz, q, sown)

    def pass_on(d):
        zz = lax.rem(z + d, chips)
        core_copy(zz).wait_recv()
        for i in range(blocks):
            sown[zz, i] = (
                sown[zz, i].astype(jnp.float32) + score[zz, i].astype(jnp.float32)
            ).astype(jnp.bfloat16)
        part_to(d).start()

    for t, d in enumerate(far):
        collect(lax.rem(z + d, chips))
        if t > 0:
            pass_on(far[t - 1])
    collect(z)
    pass_on(far[-1])

    for d in range(1, chips):
        gw_from(d).wait_recv()
    gw_sum = gw_chip[0].astype(jnp.float32)
    for zz in range(1, chips):
        gw_sum = gw_sum + gw_chip[zz].astype(jnp.float32)
    gw_out[q] = gw_sum * scale
    gw_share = remote(gw_out.at[q], gw_out.at[q], wo_s, wo_r, sub=1 - q)
    gw_share_back = remote(gw_out.at[1 - q], gw_out.at[1 - q], wo_s, wo_r, sub=1 - q)
    gw_share.start()

    core_copy(z).wait_recv()

    for d in near:
        part_to(d).wait_recv()
    for b in range(blocks):
        here = pl.ds(b * size, size)
        grad = sown[z, b].astype(jnp.float32) + score[z, b].astype(jnp.float32)
        for d in range(1, chips):
            grad = grad + landed[d, b].astype(jnp.float32)
        gfo[:, here] = (grad * fmask[:, here].astype(jnp.float32) * 2.0).astype(jnp.bfloat16)
    gf_store = pltpu.make_async_copy(gfo, gf_hbm, out_sem.at[pairs])
    gf_store.start()
    gw_share_back.wait_recv()
    gw_stores = [
        pltpu.make_async_copy(gw_out.at[i], gw_hbm.at[pl.ds(i * mid, mid)], out_sem.at[pairs + 1 + i])
        for i in range(2)
    ]
    for copy in gw_stores:
        copy.start()

    for zz in range(chips):
        gather_core(zz, q).wait_send()
        core_copy(zz).wait_send()
    for d in range(1, chips):
        gather_to(d).wait_send()
        part_to(d).wait_send()
    for c in range(pairs):
        for d in range(1, feats):
            send_prop(c, d).wait_send()
            send_grad(c, d).wait_send()
        store_hidden(c).wait()
    gw_swap.wait_send()
    for d in range(1, chips):
        gw_to(d).wait_send()
    gw_share.wait_send()
    gf_store.wait()
    for copy in gw_stores:
        copy.wait()


def make_tables(blocks, per, cap, nbr, keep_edge, column, flags, table):
    entries, lanes = column.shape
    width = table.shape[1]
    int_ = jnp.int32
    lane = lax.broadcasted_iota(int_, (1, lanes), 1)
    row = jnp.full((1, lanes), 1 << 20, int_)
    for e in range(entries):
        name = nbr[e // per, e % per]
        column[e:e + 1, :] = jnp.full((1, lanes), name, int_)
        flags[e:e + 1, :] = jnp.full((1, lanes), keep_edge[e // per, e % per], int_)
        row = jnp.where(lane == e, name, row)
    n = column[...]
    upper = lax.broadcasted_iota(int_, (entries, lanes), 1) < lax.broadcasted_iota(
        int_, (entries, lanes), 0
    )
    twin = (n == row) & upper
    below = (lax.div(n, blocks) == lax.div(row, blocks)) & (row < n)
    rank = jnp.sum(jnp.where(below | twin, 1, 0), axis=1, keepdims=True)
    twins = jnp.sum(jnp.where(twin, 1, 0), axis=1, keepdims=True)
    n = n[:, :1]
    owner = lax.div(n, blocks)
    place = owner * cap + rank
    slot = lax.broadcasted_iota(int_, (entries, width), 1)
    index = lax.broadcasted_iota(int_, (entries, width), 0)
    hit = place == slot
    entry = jnp.sum(jnp.where(hit, index, 0), axis=0, keepdims=True)
    table[0:1, :] = jnp.clip(entry, 0, entries - 1)
    table[1:2, :] = jnp.sum(jnp.where(hit, flags[:, :1], 0), axis=0, keepdims=True)
    table[2:3, :] = jnp.sum(jnp.where(hit & (twins > 0), 1, 0), axis=0, keepdims=True)
    equal = jnp.sum(jnp.where(n == slot, 1, 0), axis=0, keepdims=True)
    upto = jnp.sum(
        jnp.where((owner == lax.div(slot, blocks)) & (n <= slot), 1, 0), axis=0, keepdims=True
    )
    table[3:4, :] = jnp.where(equal > 0, jnp.clip(upto - 1, 0, cap), cap)
    table[4:8, :] = jnp.zeros((4, width), int_)


def local(chips, features, adjacency, neighbors, edge_mask, feature_mask, weight, cotangent):
    rows_dev, half = features.shape
    blocks, per, size, _ = adjacency.shape
    owners = 2 * chips
    entries = blocks * per
    cap = entries // owners + 1
    total, hid = weight.shape
    feats = total // half
    mid = total // 2
    pairs = blocks // 2
    lanes = -(-entries // 128) * 128
    width = -(-owners * max(blocks, cap) // 128) * 128
    bf, f32 = jnp.bfloat16, jnp.float32
    smem = pl.BlockSpec(memory_space=pltpu.SMEM)
    any_ = pl.BlockSpec(memory_space=pltpu.HBM)
    dma = pltpu.SemaphoreType.DMA
    body = functools.partial(
        kernel, chips, feats, blocks, per, cap, 1.0 / math.sqrt(rows_dev * owners)
    )
    hidden, grad_weight, grad_features = pl.pallas_call(
        body,
        out_shape=(
            jax.ShapeDtypeStruct((rows_dev, hid), bf),
            jax.ShapeDtypeStruct((total, hid), f32),
            jax.ShapeDtypeStruct((half, rows_dev), bf),
        ),
        in_specs=[smem] * 2 + [any_] * 5,
        out_specs=(any_, any_, any_),
        scratch_shapes=[
            pltpu.VMEM((half, rows_dev), bf),
            pltpu.VMEM((half, rows_dev), jnp.int32),
            pltpu.VMEM(adjacency.shape, bf),
            pltpu.VMEM((feats, half, hid), bf),
            pltpu.VMEM((rows_dev, hid), bf),
            pltpu.VMEM((rows_dev, hid), bf),
            pltpu.VMEM((half, rows_dev), bf),
            pltpu.VMEM((owners * blocks, half, size), bf),
            pltpu.VMEM((feats, blocks, half, size), bf),
            pltpu.VMEM((blocks, half, size), f32),
            pltpu.VMEM((feats, blocks, half, size), bf),
            pltpu.VMEM((feats, blocks, half, size), bf),
            pltpu.VMEM((entries, half, size), f32),
            pltpu.VMEM((cap + 1, half, size), f32),
        ]
        + [pltpu.VMEM((chips, blocks, half, size), bf)] * 4
        + [
            pltpu.VMEM((2, mid, hid), f32),
            pltpu.VMEM((mid, hid), f32),
            pltpu.VMEM((mid, hid), f32),
            pltpu.VMEM((chips, mid, hid), bf),
            pltpu.VMEM((2, mid, hid), f32),
            pltpu.VMEM((entries, lanes), jnp.int32),
            pltpu.VMEM((entries, lanes), jnp.int32),
            pltpu.VMEM((8, width), jnp.int32),
            pltpu.SMEM((8, width), jnp.int32),
            dma,
            dma((4 + feats,)),
            dma((pairs + 3,)),
        ]
        + [dma((chips,))] * 4
        + [dma((feats, pairs))] * 4
        + [dma((chips,))] * 4
        + [dma, dma, dma((chips,)), dma((chips,)), dma, dma],
        compiler_params=pltpu.CompilerParams(
            collective_id=0, has_side_effects=True, vmem_limit_bytes=62 * 1024 * 1024
        ),
    )(neighbors, edge_mask, features.T, feature_mask.T, adjacency, weight, cotangent)
    return hidden, grad_weight, grad_features.T


def solution(mesh):
    split = ("grp", "node", "sub")
    in_specs = (
        P(split, "feat"),
        P(split, None, None, None),
        P(split, None),
        P(split, None),
        P(split, "feat"),
        P(None, "feat"),
        P(split, "feat"),
    )
    out_specs = (P(split, "feat"), P("grp", "feat"), P(split, "feat"))
    return jax.shard_map(
        functools.partial(local, mesh.shape["node"]),
        mesh=mesh, in_specs=in_specs, out_specs=out_specs, check_vma=False,
    )
```
